32 devices in a mesh: wide: 8 (over y, x, core), narrow: 4 (over z).
Axes of the slice: x: 2, y: 2, z: 4, core: 2. Of those that a mesh axis runs over, the one named last changes fastest.
Arguments:
- hidden: bfloat16 [4096, 14336], P('narrow', 'wide'), may hold values from -6 to 6
- out_grad: bfloat16 [4096, 4096], P('wide', 'narrow'), may hold values from -6 to 6
- sign_bits: int32 [14336, 4096], P('wide', 'narrow'), may hold values 0 or 1
- pick_rows: int32 [8192], replicated, may hold values from 0 to 14335
- pick_cols: int32 [8192], replicated, may hold values from 0 to 4095
Outputs:
- sketch: float32 [2, 8192], replicated
The draws below stay inside these ranges and needn't reach their ends.
All inputs are finite; a program needn't handle non-finite values. No bound on the sum of `sign_bits` on one device may be relied on, other than what follows from the above.
Results may differ from the reference program's by a relative error of at most 0.0003.
Values may be sent and summed in bfloat16 or wider, within the bound.
No kernel may reach another device: no remote copies, remote signals or barrier semaphores. Data moves between devices by JAX's collectives and lax.ppermute only.
A program may use at most 128 MiB of HBM per device.

```python
import math
import jax
import jax.numpy as jnp

D = 4096
FF = 14336
EXAMPLES = 2
SEQ = 2048
GROUPS = 16
BAND = 128
SKETCH = 8192
TOKENS = 4096


def place_ends(result, rng, low, high):
    longest = result.shape.index(max(result.shape))
    spots = []
    for shift in (0, 1):
        where = [jax.random.randint(jax.random.fold_in(rng, axis), (), 0, length) for axis, length in enumerate(result.shape)]
        where[longest] = (where[longest] + shift) % result.shape[longest]
        spots.append(tuple(where))
    return result.at[spots[0]].set(low).at[spots[1]].set(high)


def level_of(rng, dims, shards, smallest, largest):
    def one(axis_at, shards_of):
        steps = jax.random.uniform(jax.random.fold_in(jax.random.fold_in(rng, 6), axis_at), (shards_of,), jnp.float32, smallest / len(shards), largest / len(shards))
        return jnp.repeat(jnp.exp(steps), dims[axis_at] // shards_of).reshape((-1,) + (1,) * (len(dims) - axis_at - 1))

    factor_of = one(*shards[0])
    for cut in shards[1:]:
        factor_of = factor_of * one(*cut)
    return factor_of


def centred(own_key, shape, scale, most, cuts=(), kind=jnp.bfloat16):
    gain = level_of(own_key, shape, cuts, -0.22, 0.18) if cuts else 1.0
    entries = jax.random.normal(own_key, shape, jnp.float32) * scale * gain
    return jnp.minimum(jnp.maximum(entries, -most), most).astype(kind)


def setup_inputs(seed: int = 0) -> dict:
    seeds = jax.random.split(jax.random.key(seed), 6)
    return {
        "hidden": centred(seeds[0], (TOKENS, FF), 1.0, 6.0, ((0, 4), (1, 8))),
        "out_grad": centred(seeds[1], (TOKENS, D), 1.0, 6.0, ((0, 8), (1, 4))),
        "sign_bits": place_ends((jax.random.randint(seeds[2], (FF, D), 0, 2) < 1).astype(jnp.int32), jax.random.fold_in(seeds[2], 1), 0, 1),
        "pick_rows": place_ends(jax.random.randint(seeds[3], (SKETCH,), 0, FF), jax.random.fold_in(seeds[3], 1), 0, FF - 1).astype(jnp.int32),
        "pick_cols": place_ends(jax.random.randint(seeds[4], (SKETCH,), 0, D), jax.random.fold_in(seeds[4], 1), 0, D - 1).astype(jnp.int32),
    }


def walsh_last(values):
    length = values.shape[-1]
    leading = values.shape[:-1]
    stride = 1
    while stride < length:
        pieces = values.reshape(leading + (length // (2 * stride), 2, stride))
        upper_half = pieces[..., 0, :]
        lower_half = pieces[..., 1, :]
        values = jnp.stack([upper_half + lower_half, upper_half - lower_half], axis=-2).reshape(leading + (length,))
        stride = stride * 2
    return values

def reference(hidden, out_grad, sign_bits, pick_rows, pick_cols):
    flips = (2 * sign_bits - 1).astype(jnp.float32)
    middle = FF // (GROUPS * BAND)
    factor = 1.0 / math.sqrt(GROUPS * BAND * D * SEQ)
    results = []
    for example in range(EXAMPLES):
        activations = hidden[example * SEQ:(example + 1) * SEQ]
        gradients = out_grad[example * SEQ:(example + 1) * SEQ]
        gradient = jnp.dot(activations.T, gradients, preferred_element_type=jnp.float32)
        flipped = gradient * flips
        columns = walsh_last(flipped)
        blocks = columns.reshape(GROUPS, middle, BAND, D)
        blocks = jnp.moveaxis(walsh_last(jnp.moveaxis(blocks, 0, -1)), -1, 0)
        blocks = jnp.moveaxis(walsh_last(jnp.moveaxis(blocks, 2, -1)), -1, 2)
        whole = blocks.reshape(FF, D)
        results.append(whole[pick_rows, pick_cols] * factor)
    return jnp.stack(results)
```

```python
import functools
import math

import jax
import jax.numpy as jnp
from jax import lax
from jax.experimental import pallas as pl
from jax.experimental.pallas import tpu as pltpu
from jax.sharding import PartitionSpec as P

EXAMPLES = 2
SEQ = 2048
GROUPS = 16
BAND = 128
LANES = 128


def bit_parity(value, count):
    total = jnp.zeros_like(value)
    for bit_num in range(count):
        total = total + jnp.bitwise_and(jnp.right_shift(value, bit_num), 1)
    return total % 2


def two_parts(value):
    high = value.astype(jnp.bfloat16)
    low = (value - high.astype(jnp.float32)).astype(jnp.bfloat16)
    return high, low


def dot(left, right):
    return jnp.dot(left, right, preferred_element_type=jnp.float32)


def piece_kernel(blocks, groups, grad_counts, scalars, *refs):
    refs = list(refs)
    take = lambda count: [refs.pop(0) for _ in range(count)]
    parts, found, *sample_scratch, arrived = refs[-7:]
    sides = len(grad_counts)
    acts = [take(groups) for _ in range(blocks)]
    grads = [take(count) for count in grad_counts]
    signs = [take(groups) for _ in range(sides)]
    sample_refs = take(4)
    (out,) = take(1)
    row_signs, col_signs, spots, lines = sample_scratch
    rows = groups * BAND
    cols = parts.shape[0] // sides
    picks = row_signs.shape[1]
    span_cols = min(4 * LANES, picks)
    step = pl.program_id(0)
    copies = [
        pltpu.make_async_copy(source, target, arrived.at[number])
        for number, (source, target) in enumerate(zip(sample_refs, sample_scratch))
    ]

    @pl.when((step == 0) & (scalars[0] != 0))
    def _():
        for copy in copies:
            copy.start()

    @pl.when(step == 0)
    def _():
        out[...] = jnp.zeros_like(out)

    @pl.when(scalars[0] != 0)
    def _():
        for side in range(sides):
            left = jnp.concatenate([ref[...] for ref in grads[side]], axis=1)
            right = [jnp.concatenate([ref[...] for ref in block], axis=1) for block in acts]
            total = dot(left, jnp.concatenate(right, axis=0))
            flips = []
            for ref in signs[side]:
                flip = ref[...].astype(jnp.float32)
                flips.append((2 * flip - 1 if ref.dtype == jnp.int32 else flip).T)
            high, low = two_parts(total * jnp.concatenate(flips, axis=1))
            parts[side * cols : (side + 1) * cols, :rows] = high
            parts[side * cols : (side + 1) * cols, rows:] = low

    @pl.when((step == 0) & (scalars[0] != 0))
    def _():
        for copy in copies:
            copy.wait()

    @pl.when(scalars[0] != 0)
    def _():
        begin = scalars[1 + step]
        end = scalars[2 + step]

        def sample(at, carry):
            first = pl.multiple_of(at * span_cols, span_cols)
            span = pl.ds(first, span_cols)
            right = jnp.concatenate([row_signs[:, span]] * 2, axis=0)

            def sign_of(bit):
                return col_signs[pl.ds(8 + bit - 3, 1), span]

            def join(levels, value, place, bit):
                while place & 1:
                    value = levels.pop() + sign_of(bit) * value
                    place, bit = place >> 1, bit + 1
                levels.append(value)

            outer = []
            for side in range(sides):
                values = dot(parts[side * cols : (side + 1) * cols, :], right)
                for place in range(cols // 8):
                    join(outer, values[place * 8 : place * 8 + 8], side * cols // 8 + place, 3)
            (value,) = outer
            value = jnp.sum(value * col_signs[:8, span], axis=0, keepdims=True)
            places = first + lax.broadcasted_iota(jnp.int32, (1, span_cols), 1)
            inside = (places >= begin) & (places < end)
            found[:, span] = jnp.where(inside, value, found[:, span])
            return carry

        lax.fori_loop(begin // span_cols, (end + span_cols - 1) // span_cols, sample, 0)

        @pl.when(step == pl.num_programs(0) - 1)
        def _():
            start = scalars[1]
            wide_cols = min(8 * LANES, picks)

            def spread(at, carry):
                first = pl.multiple_of(at * wide_cols, wide_cols)
                span = pl.ds(first, wide_cols)
                places = first + lax.broadcasted_iota(jnp.int32, (1, wide_cols), 1)
                inside = (places >= start) & (places < end)
                value = jnp.where(inside, found[:, span], 0.0)
                value = lines[:, span].astype(jnp.float32) * value
                high, low = two_parts(value)
                out[...] += dot(high, spots[span, :]) + dot(low, spots[span, :])
                return carry

            lax.fori_loop(start // wide_cols, (end + wide_cols - 1) // wide_cols, spread, 0)


def piece(steps, groups, scalars, acts, grads, signs, samples):
    sides = len(signs)
    cols = signs[0][0].shape[1]
    rows = groups * BAND
    picks = samples[0].shape[1]
    operands, specs = [], []

    def column_map(row_block, middle, first, group, step, scalars):
        return row_block, group * middle + first + step * scalars[0]

    for array, depth, row_block, middle, first in acts:
        for group in range(groups):
            operands.append(array)
            specs.append(
                pl.BlockSpec(
                    (depth, BAND), functools.partial(column_map, row_block, middle, first, group)
                )
            )

    def fixed_map(row_block, step, scalars):
        if isinstance(row_block, tuple):
            row_block = scalars[row_block[0]] + row_block[1]
        return row_block, 0

    once = pl.Buffered(1)
    for per_side in grads:
        for array, depth, row_block in per_side:
            operands.append(array)
            specs.append(
                pl.BlockSpec(
                    (cols, depth), functools.partial(fixed_map, row_block), pipeline_mode=once
                )
            )

    def row_map(middle, first, group, step, scalars):
        return group * middle + first + step * scalars[0], 0

    for array, middle, first in signs:
        for group in range(groups):
            operands.append(array)
            specs.append(
                pl.BlockSpec((BAND, cols), functools.partial(row_map, middle, first, group))
            )
    for array in samples:
        operands.append(array)
        specs.append(pl.BlockSpec(memory_space=pl.ANY))
    depth = sum(act[1] for act in acts)
    work = rows * cols * sides
    return pl.pallas_call(
        functools.partial(piece_kernel, len(acts), groups, [len(each) for each in grads]),
        grid_spec=pltpu.PrefetchScalarGridSpec(
            num_scalar_prefetch=1,
            grid=(steps,),
            in_specs=specs,
            out_specs=pl.BlockSpec((picks // LANES, LANES), functools.partial(fixed_map, 0)),
            scratch_shapes=[
                pltpu.VMEM((sides * cols, 2 * rows), jnp.bfloat16),
                pltpu.VMEM((1, picks), jnp.float32),
                *[pltpu.VMEM(array.shape, array.dtype) for array in samples],
                pltpu.SemaphoreType.DMA((len(samples),)),
            ],
        ),
        out_shape=jax.ShapeDtypeStruct((picks // LANES, LANES), jnp.float32),
        compiler_params=pltpu.CompilerParams(vmem_limit_bytes=48 * 1024 * 1024),
        cost_estimate=pl.CostEstimate(flops=1, bytes_accessed=1, transcendentals=0),
    )(scalars, *operands)


def after(value, *earlier):
    return lax.optimization_barrier((value, *earlier))[0]


def middle_slice(array, axis, groups, middle, first, count):
    cuts = []
    for group in range(groups):
        start = (group * middle + first) * BAND
        cuts.append(lax.slice_in_dim(array, start, start + count * BAND, axis=axis))
    return jnp.concatenate(cuts, axis=axis)


def sum_over(value, axis):
    size = lax.axis_size(axis)
    stride = 1
    while stride < size:
        pairs = [(index, index ^ stride) for index in range(size)]
        value = value + lax.ppermute(value, axis, pairs)
        stride = stride * 2
    return value


def ordered_samples(pick_rows, pick_cols, rows_local, cols_local, groups, middle):
    picks = pick_rows.shape[0]
    rows = groups * BAND
    row_here = pick_rows % rows_local
    pick_middle = row_here // BAND % middle
    row_place = row_here // (middle * BAND) * BAND + row_here % BAND
    col_place = pick_cols % (2 * cols_local)
    numbers = lax.iota(jnp.int32, picks)
    key, payload = lax.sort(
        (pick_middle * picks + numbers, row_place * (2 * cols_local) + col_place), num_keys=1
    )
    numbers = key % picks
    col_place = payload % (2 * cols_local)
    row_place = payload // (2 * cols_local)
    heads = lax.iota(jnp.int32, middle + 1)
    starts = jnp.sum((pick_middle[None, :] < heads[:, None]).astype(jnp.int32), axis=1)

    def signs(counted, kind):
        return (1 - 2 * (lax.population_count(counted) & 1)).astype(kind)

    row_signs = signs(row_place[None, :] & lax.iota(jnp.int32, rows)[:, None], jnp.bfloat16)
    bits = (2 * cols_local).bit_length() - 1
    masks = list(range(8)) + [1 << bit for bit in range(3, bits)]
    masks = jnp.array(masks + [0] * (-len(masks) % 8), jnp.int32)
    col_signs = signs(col_place[None, :] & masks[:, None], jnp.float32)
    lanes = lax.iota(jnp.int32, LANES)
    spots = (numbers[:, None] % LANES == lanes[None, :]).astype(jnp.bfloat16)
    lines = lax.iota(jnp.int32, picks // LANES)
    lines = (numbers[None, :] // LANES == lines[:, None]).astype(jnp.bfloat16)
    return (row_signs, col_signs, spots, lines), starts


def shards(hidden, out_grad, sign_bits, pick_rows, pick_cols):
    wide_count = lax.axis_size("wide")
    narrow_count = lax.axis_size("narrow")
    wide_index = lax.axis_index("wide")
    narrow_index = lax.axis_index("narrow")
    rows_local = hidden.shape[1]
    cols_local = out_grad.shape[1]
    tokens_local = hidden.shape[0]
    picks = pick_rows.shape[0]
    groups = GROUPS // wide_count
    rows = groups * BAND
    middle = rows_local // rows
    half = wide_count // EXAMPLES
    line = narrow_count == 4 and tokens_local * 2 == SEQ and half * 2 == wide_count

    samples, starts = ordered_samples(
        pick_rows, pick_cols, rows_local, cols_local, groups, middle
    )

    def scalars(active, first, count, *indices):
        parts = [jnp.int32(active)[None], starts[first : first + count + 1]]
        return jnp.concatenate(parts + [index[None] for index in indices])

    if line:
        partner = [(0, 1), (1, 0), (2, 3), (3, 2)]
        inner = [(1, 2), (2, 1)]
        inward = [(0, 1), (3, 2)]
        outward = [(1, 0), (2, 3)]
        split = middle // 2
        near = narrow_index // 2
        is_inner = ((narrow_index == 1) | (narrow_index == 2)).astype(jnp.int32)

        all_grads = lax.all_gather(out_grad.T, "wide", axis=0, tiled=True)
        tokens = out_grad.shape[0]
        depth = out_grad.shape[0] // 2
        swaps = [[], []]
        for z in range(4):
            for w in range(half):
                source = (half * (1 - z // 2) + w) * 4 + z
                for part in range(2):
                    swaps[part].append((source, (2 * w + part) * 4 + z))
        first_part = lax.ppermute(out_grad[:depth], ("wide", "narrow"), swaps[0])
        second_part = lax.ppermute(out_grad[depth:], ("wide", "narrow"), swaps[1])
        share = jnp.where(wide_index % 2 == 0, first_part, second_part).T

        def far_signs(first, count):
            cut = middle_slice(sign_bits, 0, groups, middle, first, count)
            return (2 * cut - 1).astype(jnp.bfloat16)

        def send(value, pairs, *earlier):
            return lax.ppermute(after(value, *earlier), "narrow", pairs)

        mid = send(hidden, inner)
        paired = send(hidden, partner)
        share = send(share, inward)
        shared = lax.all_gather(share, "wide", axis=0, tiled=True)

        def paired_part(first, count):
            return middle_slice(paired, 1, groups, middle, first, count)

        second = send(paired_part(0, split), inner)
        far_cuts = [(split, middle - 2 - split), (middle - 2, 1), (middle - 1, 1)]
        seconds = [send(paired_part(*cut), inner) for cut in far_cuts]
        flips = send(far_signs(split, middle - split), inward, paired)

        shared_tokens = share.shape[1]

        def token_blocks(array, indices):
            tokens = array.shape[1]
            return [
                (array, tokens, (index, part))
                for index in indices
                for part in range(tokens_local // tokens)
            ]

        def first_of(tokens, block):
            return block * (tokens_local // tokens)

        near_sum = piece(
            middle,
            groups,
            scalars(
                1,
                0,
                middle,
                first_of(tokens, narrow_index),
                first_of(tokens, narrow_index ^ 1),
            ),
            [(hidden, tokens_local, 0, middle, 0), (paired, tokens_local, 0, middle, 0)],
            [token_blocks(all_grads, (middle + 2, middle + 3))],
            [(sign_bits, middle, 0)],
            samples,
        )

        far_one = 2 - near
        far_two = far_one ^ 1

        far_at = [
            first_of(tokens, far_one),
            first_of(tokens, far_two),
            first_of(shared_tokens, far_one % 2),
            first_of(shared_tokens, far_two % 2),
        ]

        def own_far_piece(active, one, two):
            return piece(
                split,
                groups,
                scalars(active, 0, split, *far_at[:2]),
                [
                    (one, tokens_local, 0, one.shape[1] // rows, 0),
                    (two, tokens_local, 0, split, 0),
                ],
                [token_blocks(all_grads, (split + 2, split + 3))],
                [(sign_bits, middle, 0)],
                samples,
            )

        def far_piece(first, count, received, flips):
            at = count + 2
            return piece(
                count,
                groups,
                scalars(is_inner, first, count, *far_at),
                [
                    (mid, tokens_local, 0, middle, first),
                    (received, tokens_local, 0, count, 0),
                ],
                [
                    token_blocks(all_grads, (at, at + 1)),
                    token_blocks(shared, (at + 2, at + 3)),
                ],
                [(sign_bits, middle, first), (flips, middle - split, first - split)],
                samples,
            )

        second = after(second, near_sum)
        end_one = send(middle_slice(mid, 1, groups, middle, 0, split), outward, near_sum)
        end_two = send(second, outward)
        far_sums = [own_far_piece(is_inner, mid, second)]
        for index, cut in enumerate(far_cuts):
            done = far_sums[-1]
            if index == len(far_cuts) - 1:
                one, two = after(end_one, done), after(end_two, done)
                far_sums.append(own_far_piece(1 - is_inner, one, two))
                done = far_sums[-1]
            far_sums.append(far_piece(*cut, after(seconds[index], done), after(flips, done)))
        far_sum = functools.reduce(jnp.add, far_sums)
        sums = jnp.where(
            near == 0, jnp.stack([near_sum, far_sum]), jnp.stack([far_sum, near_sum])
        )
    else:
        acts_all = lax.all_gather(hidden, "narrow", axis=0, tiled=True)
        all_grads = lax.all_gather(out_grad.T, "wide", axis=0, tiled=True)
        tokens = out_grad.shape[0]
        sums = jnp.stack(
            [
                piece(
                    middle,
                    groups,
                    scalars(1, 0, middle),
                    [(acts_all, SEQ, example, middle, 0)],
                    [
                        [
                            (all_grads, tokens, example * (SEQ // tokens) + part)
                            for part in range(SEQ // tokens)
                        ]
                    ],
                    [(sign_bits, middle, 0)],
                    samples,
                )
                for example in range(EXAMPLES)
            ]
        )
    parity = bit_parity(
        jnp.bitwise_and(pick_rows // rows_local, wide_index), wide_count.bit_length() - 1
    ) + bit_parity(
        jnp.bitwise_and(pick_cols // cols_local, narrow_index), narrow_count.bit_length() - 1
    )
    scale = 1.0 / math.sqrt(GROUPS * BAND * cols_local * narrow_count * SEQ)
    weights = (1 - 2 * (parity % 2)).astype(jnp.float32) * scale
    terms = sums.reshape(EXAMPLES, picks) * weights[None]
    return sum_over(sum_over(terms, "wide"), "narrow")


def solution(mesh):
    placed = (P("narrow", "wide"), P("wide", "narrow"), P("wide", "narrow"), P(), P())
    return jax.shard_map(shards, mesh=mesh, in_specs=placed, out_specs=P(), check_vma=False)
```

```python
import functools
import math

import jax
import jax.numpy as jnp
from jax import lax
from jax.experimental import pallas as pl
from jax.experimental.pallas import tpu as pltpu
from jax.sharding import PartitionSpec as P

EXAMPLES = 2
SEQ = 2048
GROUPS = 16
BAND = 128
LANES = 128


def bit_parity(value, count):
    total = jnp.zeros_like(value)
    for bit_num in range(count):
        total = total + jnp.bitwise_and(jnp.right_shift(value, bit_num), 1)
    return total % 2


def two_parts(value):
    high = value.astype(jnp.bfloat16)
    low = (value - high.astype(jnp.float32)).astype(jnp.bfloat16)
    return high, low


def dot(left, right):
    return jnp.dot(left, right, preferred_element_type=jnp.float32)


def piece_kernel(blocks, groups, grad_counts, scalars, *refs):
    refs = list(refs)
    take = lambda count: [refs.pop(0) for _ in range(count)]
    parts, found, *sample_scratch, arrived = refs[-7:]
    sides = len(grad_counts)
    acts = [take(groups) for _ in range(blocks)]
    grads = [take(count) for count in grad_counts]
    signs = [take(groups) for _ in range(sides)]
    sample_refs = take(4)
    (out,) = take(1)
    row_signs, col_signs, spots, lines = sample_scratch
    rows = groups * BAND
    cols = parts.shape[0] // sides
    picks = row_signs.shape[1]
    span_cols = min(4 * LANES, picks)
    step = pl.program_id(0)
    copies = [
        pltpu.make_async_copy(source, target, arrived.at[number])
        for number, (source, target) in enumerate(zip(sample_refs, sample_scratch))
    ]

    @pl.when((step == 0) & (scalars[0] != 0))
    def _():
        for copy in copies:
            copy.start()

    @pl.when(step == 0)
    def _():
        out[...] = jnp.zeros_like(out)

    @pl.when(scalars[0] != 0)
    def _():
        for side in range(sides):
            left = jnp.concatenate([ref[...] for ref in grads[side]], axis=1)
            right = [jnp.concatenate([ref[...] for ref in block], axis=1) for block in acts]
            total = dot(left, jnp.concatenate(right, axis=0))
            flips = []
            for ref in signs[side]:
                flip = ref[...].astype(jnp.float32)
                flips.append((2 * flip - 1 if ref.dtype == jnp.int32 else flip).T)
            high, low = two_parts(total * jnp.concatenate(flips, axis=1))
            parts[side * cols : (side + 1) * cols, :rows] = high
            parts[side * cols : (side + 1) * cols, rows:] = low

    @pl.when((step == 0) & (scalars[0] != 0))
    def _():
        for copy in copies:
            copy.wait()

    @pl.when(scalars[0] != 0)
    def _():
        begin = scalars[1 + step]
        end = scalars[2 + step]

        def sample(at, carry):
            first = pl.multiple_of(at * span_cols, span_cols)
            span = pl.ds(first, span_cols)
            right = jnp.concatenate([row_signs[:, span]] * 2, axis=0)

            def sign_of(bit):
                return col_signs[pl.ds(8 + bit - 3, 1), span]

            def join(levels, value, place, bit):
                while place & 1:
                    value = levels.pop() + sign_of(bit) * value
                    place, bit = place >> 1, bit + 1
                levels.append(value)

            outer = []
            for side in range(sides):
                values = dot(parts[side * cols : (side + 1) * cols, :], right)
                for place in range(cols // 8):
                    join(outer, values[place * 8 : place * 8 + 8], side * cols // 8 + place, 3)
            (value,) = outer
            value = jnp.sum(value * col_signs[:8, span], axis=0, keepdims=True)
            places = first + lax.broadcasted_iota(jnp.int32, (1, span_cols), 1)
            inside = (places >= begin) & (places < end)
            found[:, span] = jnp.where(inside, value, found[:, span])
            return carry

        lax.fori_loop(begin // span_cols, (end + span_cols - 1) // span_cols, sample, 0)

        @pl.when(step == pl.num_programs(0) - 1)
        def _():
            start = scalars[1]
            wide_cols = min(8 * LANES, picks)

            def spread(at, carry):
                first = pl.multiple_of(at * wide_cols, wide_cols)
                span = pl.ds(first, wide_cols)
                places = first + lax.broadcasted_iota(jnp.int32, (1, wide_cols), 1)
                inside = (places >= start) & (places < end)
                value = jnp.where(inside, found[:, span], 0.0)
                value = lines[:, span].astype(jnp.float32) * value
                high, low = two_parts(value)
                out[...] += dot(high, spots[span, :]) + dot(low, spots[span, :])
                return carry

            lax.fori_loop(start // wide_cols, (end + wide_cols - 1) // wide_cols, spread, 0)


def piece(steps, groups, scalars, acts, grads, signs, samples):
    sides = len(signs)
    cols = signs[0][0].shape[1]
    rows = groups * BAND
    picks = samples[0].shape[1]
    operands, specs = [], []

    def column_map(row_block, middle, first, group, step, scalars):
        return row_block, group * middle + first + step * scalars[0]

    for array, depth, row_block, middle, first in acts:
        for group in range(groups):
            operands.append(array)
            specs.append(
                pl.BlockSpec(
                    (depth, BAND), functools.partial(column_map, row_block, middle, first, group)
                )
            )

    def fixed_map(row_block, step, scalars):
        if isinstance(row_block, tuple):
            row_block = scalars[row_block[0]] + row_block[1]
        return row_block, 0

    once = pl.Buffered(1)
    for per_side in grads:
        for array, depth, row_block in per_side:
            operands.append(array)
            specs.append(
                pl.BlockSpec(
                    (cols, depth), functools.partial(fixed_map, row_block), pipeline_mode=once
                )
            )

    def row_map(middle, first, group, step, scalars):
        return group * middle + first + step * scalars[0], 0

    for array, middle, first in signs:
        for group in range(groups):
            operands.append(array)
            specs.append(
                pl.BlockSpec((BAND, cols), functools.partial(row_map, middle, first, group))
            )
    for array in samples:
        operands.append(array)
        specs.append(pl.BlockSpec(memory_space=pl.ANY))
    depth = sum(act[1] for act in acts)
    work = rows * cols * sides
    return pl.pallas_call(
        functools.partial(piece_kernel, len(acts), groups, [len(each) for each in grads]),
        grid_spec=pltpu.PrefetchScalarGridSpec(
            num_scalar_prefetch=1,
            grid=(steps,),
            in_specs=specs,
            out_specs=pl.BlockSpec((picks // LANES, LANES), functools.partial(fixed_map, 0)),
            scratch_shapes=[
                pltpu.VMEM((sides * cols, 2 * rows), jnp.bfloat16),
                pltpu.VMEM((1, picks), jnp.float32),
                *[pltpu.VMEM(array.shape, array.dtype) for array in samples],
                pltpu.SemaphoreType.DMA((len(samples),)),
            ],
        ),
        out_shape=jax.ShapeDtypeStruct((picks // LANES, LANES), jnp.float32),
        compiler_params=pltpu.CompilerParams(vmem_limit_bytes=48 * 1024 * 1024),
        cost_estimate=pl.CostEstimate(
            flops=8 * steps * work * depth, bytes_accessed=work, transcendentals=0
        ),
    )(scalars, *operands)


def after(value, *earlier):
    return lax.optimization_barrier((value, *earlier))[0]


def middle_slice(array, axis, groups, middle, first, count):
    cuts = []
    for group in range(groups):
        start = (group * middle + first) * BAND
        cuts.append(lax.slice_in_dim(array, start, start + count * BAND, axis=axis))
    return jnp.concatenate(cuts, axis=axis)


def sum_over(value, axis):
    size = lax.axis_size(axis)
    stride = 1
    while stride < size:
        pairs = [(index, index ^ stride) for index in range(size)]
        value = value + lax.ppermute(value, axis, pairs)
        stride = stride * 2
    return value


def ordered_samples(pick_rows, pick_cols, rows_local, cols_local, groups, middle):
    picks = pick_rows.shape[0]
    rows = groups * BAND
    row_here = pick_rows % rows_local
    pick_middle = row_here // BAND % middle
    row_place = row_here // (middle * BAND) * BAND + row_here % BAND
    col_place = pick_cols % (2 * cols_local)
    numbers = lax.iota(jnp.int32, picks)
    key, payload = lax.sort(
        (pick_middle * picks + numbers, row_place * (2 * cols_local) + col_place), num_keys=1
    )
    numbers = key % picks
    col_place = payload % (2 * cols_local)
    row_place = payload // (2 * cols_local)
    heads = lax.iota(jnp.int32, middle + 1)
    starts = jnp.sum((pick_middle[None, :] < heads[:, None]).astype(jnp.int32), axis=1)

    def signs(counted, kind):
        return (1 - 2 * (lax.population_count(counted) & 1)).astype(kind)

    row_signs = signs(row_place[None, :] & lax.iota(jnp.int32, rows)[:, None], jnp.bfloat16)
    bits = (2 * cols_local).bit_length() - 1
    masks = list(range(8)) + [1 << bit for bit in range(3, bits)]
    masks = jnp.array(masks + [0] * (-len(masks) % 8), jnp.int32)
    col_signs = signs(col_place[None, :] & masks[:, None], jnp.float32)
    lanes = lax.iota(jnp.int32, LANES)
    spots = (numbers[:, None] % LANES == lanes[None, :]).astype(jnp.bfloat16)
    lines = lax.iota(jnp.int32, picks // LANES)
    lines = (numbers[None, :] // LANES == lines[:, None]).astype(jnp.bfloat16)
    return (row_signs, col_signs, spots, lines), starts


def shards(hidden, out_grad, sign_bits, pick_rows, pick_cols):
    wide_count = lax.axis_size("wide")
    narrow_count = lax.axis_size("narrow")
    wide_index = lax.axis_index("wide")
    narrow_index = lax.axis_index("narrow")
    rows_local = hidden.shape[1]
    cols_local = out_grad.shape[1]
    tokens_local = hidden.shape[0]
    picks = pick_rows.shape[0]
    groups = GROUPS // wide_count
    rows = groups * BAND
    middle = rows_local // rows
    half = wide_count // EXAMPLES
    line = narrow_count == 4 and tokens_local * 2 == SEQ and half * 2 == wide_count

    samples, starts = ordered_samples(
        pick_rows, pick_cols, rows_local, cols_local, groups, middle
    )

    def scalars(active, first, count, *indices):
        parts = [jnp.int32(active)[None], starts[first : first + count + 1]]
        return jnp.concatenate(parts + [index[None] for index in indices])

    if line:
        partner = [(0, 1), (1, 0), (2, 3), (3, 2)]
        inner = [(1, 2), (2, 1)]
        inward = [(0, 1), (3, 2)]
        near = narrow_index // 2
        is_inner = ((narrow_index == 1) | (narrow_index == 2)).astype(jnp.int32)

        all_grads = lax.all_gather(out_grad.T, "wide", axis=0, tiled=True)
        tokens = out_grad.shape[0]
        depth = out_grad.shape[0] // 2
        swaps = [[], []]
        for z in range(4):
            for w in range(half):
                source = (half * (1 - z // 2) + w) * 4 + z
                for part in range(2):
                    swaps[part].append((source, (2 * w + part) * 4 + z))
        first_part = lax.ppermute(out_grad[:depth], ("wide", "narrow"), swaps[0])
        second_part = lax.ppermute(out_grad[depth:], ("wide", "narrow"), swaps[1])
        share = jnp.where(wide_index % 2 == 0, first_part, second_part).T

        def far_signs(first, count):
            cut = middle_slice(sign_bits, 0, groups, middle, first, count)
            return (2 * cut - 1).astype(jnp.bfloat16)

        def send(value, pairs, *earlier):
            return lax.ppermute(after(value, *earlier), "narrow", pairs)

        mid = send(hidden, inner)
        paired = after(send(hidden, partner), mid)
        share = send(share, inward)
        shared = lax.all_gather(share, "wide", axis=0, tiled=True)

        def paired_part(first, count):
            return middle_slice(paired, 1, groups, middle, first, count)

        far_cuts = [(0, 2), (2, 2), (4, middle - 4)]
        second_cuts = [(0, 4), far_cuts[2]]
        seconds = [send(paired_part(*cut), inner) for cut in second_cuts]
        flips = [send(far_signs(*cut), inward, paired) for cut in far_cuts]

        shared_tokens = share.shape[1]

        def token_blocks(array, indices):
            tokens = array.shape[1]
            return [
                (array, tokens, (index, part))
                for index in indices
                for part in range(tokens_local // tokens)
            ]

        def first_of(tokens, block):
            return block * (tokens_local // tokens)

        near_sum = piece(
            middle,
            groups,
            scalars(
                1,
                0,
                middle,
                first_of(tokens, narrow_index),
                first_of(tokens, narrow_index ^ 1),
            ),
            [(hidden, tokens_local, 0, middle, 0), (paired, tokens_local, 0, middle, 0)],
            [token_blocks(all_grads, (middle + 2, middle + 3))],
            [(sign_bits, middle, 0)],
            samples,
        )

        far_one = 2 - near
        far_two = far_one ^ 1

        far_at = [
            first_of(tokens, far_one),
            first_of(tokens, far_two),
            first_of(shared_tokens, far_one % 2),
            first_of(shared_tokens, far_two % 2),
        ]

        def far_piece(index, received, flips):
            first, count = far_cuts[index]
            second_first, second_count = second_cuts[index // 2]
            at = count + 2
            return piece(
                count,
                groups,
                scalars(is_inner, first, count, *far_at),
                [
                    (mid, tokens_local, 0, middle, first),
                    (received, tokens_local, 0, second_count, first - second_first),
                ],
                [
                    token_blocks(all_grads, (at, at + 1)),
                    token_blocks(shared, (at + 2, at + 3)),
                ],
                [(sign_bits, middle, first), (flips, count, 0)],
                samples,
            )

        far_sums = []
        done = near_sum
        for index, flip in enumerate(flips):
            received = seconds[index // 2]
            far_sums.append(far_piece(index, after(received, done), after(flip, done)))
            done = far_sums[-1]
        far_sum = functools.reduce(jnp.add, far_sums)
        sums = jnp.where(
            near == 0, jnp.stack([near_sum, far_sum]), jnp.stack([far_sum, near_sum])
        )
    else:
        acts_all = lax.all_gather(hidden, "narrow", axis=0, tiled=True)
        all_grads = lax.all_gather(out_grad.T, "wide", axis=0, tiled=True)
        tokens = out_grad.shape[0]
        sums = jnp.stack(
            [
                piece(
                    middle,
                    groups,
                    scalars(1, 0, middle),
                    [(acts_all, SEQ, example, middle, 0)],
                    [
                        [
                            (all_grads, tokens, example * (SEQ // tokens) + part)
                            for part in range(SEQ // tokens)
                        ]
                    ],
                    [(sign_bits, middle, 0)],
                    samples,
                )
                for example in range(EXAMPLES)
            ]
        )
    parity = bit_parity(
        jnp.bitwise_and(pick_rows // rows_local, wide_index), wide_count.bit_length() - 1
    ) + bit_parity(
        jnp.bitwise_and(pick_cols // cols_local, narrow_index), narrow_count.bit_length() - 1
    )
    scale = 1.0 / math.sqrt(GROUPS * BAND * cols_local * narrow_count * SEQ)
    weights = (1 - 2 * (parity % 2)).astype(jnp.float32) * scale
    terms = sums.reshape(EXAMPLES, picks) * weights[None]
    return sum_over(sum_over(terms, "wide"), "narrow")


def solution(mesh):
    placed = (P("narrow", "wide"), P("wide", "narrow"), P("wide", "narrow"), P(), P())
    return jax.shard_map(shards, mesh=mesh, in_specs=placed, out_specs=P(), check_vma=False)
```

```python
import functools
import math

import jax
import jax.numpy as jnp
from jax import lax
from jax.experimental import pallas as pl
from jax.experimental.pallas import tpu as pltpu
from jax.sharding import PartitionSpec as P

EXAMPLES = 2
SEQ = 2048
GROUPS = 16
BAND = 128
LANES = 128


def bit_parity(value, count):
    total = jnp.zeros_like(value)
    for bit_num in range(count):
        total = total + jnp.bitwise_and(jnp.right_shift(value, bit_num), 1)
    return total % 2


def two_parts(value):
    high = value.astype(jnp.bfloat16)
    low = (value - high.astype(jnp.float32)).astype(jnp.bfloat16)
    return high, low


def dot(left, right):
    return jnp.dot(left, right, preferred_element_type=jnp.float32)


def piece_kernel(blocks, groups, grad_counts, scalars, *refs):
    refs = list(refs)
    take = lambda count: [refs.pop(0) for _ in range(count)]
    parts, found, *sample_scratch, arrived = refs[-7:]
    sides = len(grad_counts)
    acts = [take(groups) for _ in range(blocks)]
    grads = [take(count) for count in grad_counts]
    signs = [take(groups) for _ in range(sides)]
    sample_refs = take(4)
    (out,) = take(1)
    row_signs, col_signs, spots, lines = sample_scratch
    rows = groups * BAND
    cols = parts.shape[0] // sides
    picks = row_signs.shape[1]
    span_cols = min(4 * LANES, picks)
    step = pl.program_id(0)
    copies = [
        pltpu.make_async_copy(source, target, arrived.at[number])
        for number, (source, target) in enumerate(zip(sample_refs, sample_scratch))
    ]

    @pl.when((step == 0) & (scalars[0] != 0))
    def _():
        for copy in copies:
            copy.start()

    @pl.when(step == 0)
    def _():
        out[...] = jnp.zeros_like(out)

    @pl.when(scalars[0] != 0)
    def _():
        for side in range(sides):
            left = jnp.concatenate([ref[...] for ref in grads[side]], axis=1)
            right = [jnp.concatenate([ref[...] for ref in block], axis=1) for block in acts]
            total = dot(left, jnp.concatenate(right, axis=0))
            flips = []
            for ref in signs[side]:
                flip = ref[...].astype(jnp.float32)
                flips.append((2 * flip - 1 if ref.dtype == jnp.int32 else flip).T)
            high, low = two_parts(total * jnp.concatenate(flips, axis=1))
            parts[side * cols : (side + 1) * cols, :rows] = high
            parts[side * cols : (side + 1) * cols, rows:] = low

    @pl.when((step == 0) & (scalars[0] != 0))
    def _():
        for copy in copies:
            copy.wait()

    @pl.when(scalars[0] != 0)
    def _():
        begin = scalars[1 + step]
        end = scalars[2 + step]

        def sample(at, carry):
            first = pl.multiple_of(at * span_cols, span_cols)
            span = pl.ds(first, span_cols)
            right = jnp.concatenate([row_signs[:, span]] * 2, axis=0)

            def sign_of(bit):
                return col_signs[pl.ds(8 + bit - 3, 1), span]

            def join(levels, value, place, bit):
                while place & 1:
                    value = levels.pop() + sign_of(bit) * value
                    place, bit = place >> 1, bit + 1
                levels.append(value)

            outer = []
            for side in range(sides):
                values = dot(parts[side * cols : (side + 1) * cols, :], right)
                for place in range(cols // 8):
                    join(outer, values[place * 8 : place * 8 + 8], side * cols // 8 + place, 3)
            (value,) = outer
            value = jnp.sum(value * col_signs[:8, span], axis=0, keepdims=True)
            places = first + lax.broadcasted_iota(jnp.int32, (1, span_cols), 1)
            inside = (places >= begin) & (places < end)
            found[:, span] = jnp.where(inside, value, found[:, span])
            return carry

        lax.fori_loop(begin // span_cols, (end + span_cols - 1) // span_cols, sample, 0)

        @pl.when(step == pl.num_programs(0) - 1)
        def _():
            start = scalars[1]
            wide_cols = min(8 * LANES, picks)

            def spread(at, carry):
                first = pl.multiple_of(at * wide_cols, wide_cols)
                span = pl.ds(first, wide_cols)
                places = first + lax.broadcasted_iota(jnp.int32, (1, wide_cols), 1)
                inside = (places >= start) & (places < end)
                value = jnp.where(inside, found[:, span], 0.0)
                value = lines[:, span].astype(jnp.float32) * value
                high, low = two_parts(value)
                out[...] += dot(high, spots[span, :]) + dot(low, spots[span, :])
                return carry

            lax.fori_loop(start // wide_cols, (end + wide_cols - 1) // wide_cols, spread, 0)


def piece(steps, groups, scalars, acts, grads, signs, samples):
    sides = len(signs)
    cols = signs[0][0].shape[1]
    rows = groups * BAND
    picks = samples[0].shape[1]
    operands, specs = [], []

    def column_map(row_block, middle, first, group, step, scalars):
        return row_block, group * middle + first + step * scalars[0]

    for array, depth, row_block, middle, first in acts:
        for group in range(groups):
            operands.append(array)
            specs.append(
                pl.BlockSpec(
                    (depth, BAND), functools.partial(column_map, row_block, middle, first, group)
                )
            )

    def fixed_map(row_block, step, scalars):
        if isinstance(row_block, tuple):
            row_block = scalars[row_block[0]] + row_block[1]
        return row_block, 0

    once = pl.Buffered(1)
    for per_side in grads:
        for array, depth, row_block in per_side:
            operands.append(array)
            specs.append(
                pl.BlockSpec(
                    (cols, depth), functools.partial(fixed_map, row_block), pipeline_mode=once
                )
            )

    def row_map(middle, first, group, step, scalars):
        return group * middle + first + step * scalars[0], 0

    for array, middle, first in signs:
        for group in range(groups):
            operands.append(array)
            specs.append(
                pl.BlockSpec((BAND, cols), functools.partial(row_map, middle, first, group))
            )
    for array in samples:
        operands.append(array)
        specs.append(pl.BlockSpec(memory_space=pl.ANY))
    depth = sum(act[1] for act in acts)
    work = rows * cols * sides
    return pl.pallas_call(
        functools.partial(piece_kernel, len(acts), groups, [len(each) for each in grads]),
        grid_spec=pltpu.PrefetchScalarGridSpec(
            num_scalar_prefetch=1,
            grid=(steps,),
            in_specs=specs,
            out_specs=pl.BlockSpec((picks // LANES, LANES), functools.partial(fixed_map, 0)),
            scratch_shapes=[
                pltpu.VMEM((sides * cols, 2 * rows), jnp.bfloat16),
                pltpu.VMEM((1, picks), jnp.float32),
                *[pltpu.VMEM(array.shape, array.dtype) for array in samples],
                pltpu.SemaphoreType.DMA((len(samples),)),
            ],
        ),
        out_shape=jax.ShapeDtypeStruct((picks // LANES, LANES), jnp.float32),
        compiler_params=pltpu.CompilerParams(vmem_limit_bytes=48 * 1024 * 1024),
        cost_estimate=pl.CostEstimate(
            flops=8 * steps * work * depth, bytes_accessed=work, transcendentals=0
        ),
    )(scalars, *operands)


def after(value, *earlier):
    return lax.optimization_barrier((value, *earlier))[0]


def middle_slice(array, axis, groups, middle, first, count):
    cuts = []
    for group in range(groups):
        start = (group * middle + first) * BAND
        cuts.append(lax.slice_in_dim(array, start, start + count * BAND, axis=axis))
    return jnp.concatenate(cuts, axis=axis)


def sum_over(value, axis):
    size = lax.axis_size(axis)
    stride = 1
    while stride < size:
        pairs = [(index, index ^ stride) for index in range(size)]
        value = value + lax.ppermute(value, axis, pairs)
        stride = stride * 2
    return value


def ordered_samples(pick_rows, pick_cols, rows_local, cols_local, groups, middle):
    picks = pick_rows.shape[0]
    rows = groups * BAND
    row_here = pick_rows % rows_local
    pick_middle = row_here // BAND % middle
    row_place = row_here // (middle * BAND) * BAND + row_here % BAND
    col_place = pick_cols % (2 * cols_local)
    numbers = lax.iota(jnp.int32, picks)
    key, payload = lax.sort(
        (pick_middle * picks + numbers, row_place * (2 * cols_local) + col_place), num_keys=1
    )
    numbers = key % picks
    col_place = payload % (2 * cols_local)
    row_place = payload // (2 * cols_local)
    heads = lax.iota(jnp.int32, middle + 1)
    starts = jnp.sum((pick_middle[None, :] < heads[:, None]).astype(jnp.int32), axis=1)

    def signs(counted, kind):
        return (1 - 2 * (lax.population_count(counted) & 1)).astype(kind)

    row_signs = signs(row_place[None, :] & lax.iota(jnp.int32, rows)[:, None], jnp.bfloat16)
    bits = (2 * cols_local).bit_length() - 1
    masks = list(range(8)) + [1 << bit for bit in range(3, bits)]
    masks = jnp.array(masks + [0] * (-len(masks) % 8), jnp.int32)
    col_signs = signs(col_place[None, :] & masks[:, None], jnp.float32)
    lanes = lax.iota(jnp.int32, LANES)
    spots = (numbers[:, None] % LANES == lanes[None, :]).astype(jnp.bfloat16)
    lines = lax.iota(jnp.int32, picks // LANES)
    lines = (numbers[None, :] // LANES == lines[:, None]).astype(jnp.bfloat16)
    return (row_signs, col_signs, spots, lines), starts


def shards(hidden, out_grad, sign_bits, pick_rows, pick_cols):
    wide_count = lax.axis_size("wide")
    narrow_count = lax.axis_size("narrow")
    wide_index = lax.axis_index("wide")
    narrow_index = lax.axis_index("narrow")
    rows_local = hidden.shape[1]
    cols_local = out_grad.shape[1]
    tokens_local = hidden.shape[0]
    picks = pick_rows.shape[0]
    groups = GROUPS // wide_count
    rows = groups * BAND
    middle = rows_local // rows
    half = wide_count // EXAMPLES
    line = narrow_count == 4 and tokens_local * 2 == SEQ and half * 2 == wide_count

    samples, starts = ordered_samples(
        pick_rows, pick_cols, rows_local, cols_local, groups, middle
    )

    def scalars(active, first, count, *indices):
        parts = [jnp.int32(active)[None], starts[first : first + count + 1]]
        return jnp.concatenate(parts + [index[None] for index in indices])

    if line:
        partner = [(0, 1), (1, 0), (2, 3), (3, 2)]
        inner = [(1, 2), (2, 1)]
        inward = [(0, 1), (3, 2)]
        near = narrow_index // 2
        is_inner = ((narrow_index == 1) | (narrow_index == 2)).astype(jnp.int32)

        all_grads = lax.all_gather(out_grad.T, "wide", axis=0, tiled=True)
        tokens = out_grad.shape[0]
        depth = out_grad.shape[0] // 2
        swaps = [[], []]
        for z in range(4):
            for w in range(half):
                source = (half * (1 - z // 2) + w) * 4 + z
                for part in range(2):
                    swaps[part].append((source, (2 * w + part) * 4 + z))
        first_part = lax.ppermute(out_grad[:depth], ("wide", "narrow"), swaps[0])
        second_part = lax.ppermute(out_grad[depth:], ("wide", "narrow"), swaps[1])
        share = jnp.where(wide_index % 2 == 0, first_part, second_part).T

        def far_signs(first, count):
            cut = middle_slice(sign_bits, 0, groups, middle, first, count)
            return (2 * cut - 1).astype(jnp.bfloat16)

        def send(value, pairs, *earlier):
            return lax.ppermute(after(value, *earlier), "narrow", pairs)

        mid = send(hidden, inner)
        paired = after(send(hidden, partner), mid)
        share = send(share, inward)
        shared = lax.all_gather(share, "wide", axis=0, tiled=True)

        def paired_part(first, count):
            return middle_slice(paired, 1, groups, middle, first, count)

        far_cuts = [(0, 2), (2, middle - 4), (middle - 2, 2)]
        near_cuts = [(0, middle - 2), (middle - 2, 2)]
        ends = [middle_slice(hidden, 1, groups, middle, *cut) for cut in near_cuts]
        mids = [send(end, inner) for end in ends]
        paired = [after(send(ends[0], partner), mids[0])]
        paired.append(send(ends[1], partner, paired[0]))

        def cut_of(index):
            first, _ = far_cuts[index]
            which = 0 if first < near_cuts[1][0] else 1
            offset, size = near_cuts[which]
            return which, size, first - offset

        def second_part(index):
            which, size, place = cut_of(index)
            return middle_slice(paired[which], 1, groups, size, place, far_cuts[index][1])

        seconds = [send(second_part(index), inner) for index in (0, 1)]
        flips = [send(far_signs(*cut), inward, paired[0]) for cut in far_cuts[:2]]

        shared_tokens = share.shape[1]

        def token_blocks(array, indices):
            tokens = array.shape[1]
            return [
                (array, tokens, (index, part))
                for index in indices
                for part in range(tokens_local // tokens)
            ]

        def first_of(tokens, block):
            return block * (tokens_local // tokens)

        def near_piece(index, received):
            first, count = near_cuts[index]
            return piece(
                count,
                groups,
                scalars(
                    1,
                    first,
                    count,
                    first_of(tokens, narrow_index),
                    first_of(tokens, narrow_index ^ 1),
                ),
                [
                    (hidden, tokens_local, 0, middle, first),
                    (received, tokens_local, 0, count, 0),
                ],
                [token_blocks(all_grads, (count + 2, count + 3))],
                [(sign_bits, middle, first)],
                samples,
            )

        near_first = near_piece(0, after(paired[0], mids[1]))
        paired[1] = after(paired[1], near_first)
        seconds.append(send(second_part(2), inner))
        flips.append(send(far_signs(*far_cuts[2]), inward, paired[1]))
        near_second = near_piece(1, paired[1])
        near_sum = near_first + near_second

        far_one = 2 - near
        far_two = far_one ^ 1

        far_at = [
            first_of(tokens, far_one),
            first_of(tokens, far_two),
            first_of(shared_tokens, far_one % 2),
            first_of(shared_tokens, far_two % 2),
        ]

        def far_piece(index, received, flips):
            first, count = far_cuts[index]
            which, size, place = cut_of(index)
            at = count + 2
            return piece(
                count,
                groups,
                scalars(is_inner, first, count, *far_at),
                [
                    (mids[which], tokens_local, 0, size, place),
                    (received, tokens_local, 0, count, 0),
                ],
                [
                    token_blocks(all_grads, (at, at + 1)),
                    token_blocks(shared, (at + 2, at + 3)),
                ],
                [(sign_bits, middle, first), (flips, count, 0)],
                samples,
            )

        far_sums = []
        done = near_second
        for index, flip in enumerate(flips):
            received = after(seconds[index], done)
            far_sums.append(far_piece(index, received, after(flip, done)))
            done = far_sums[-1]
        far_sum = functools.reduce(jnp.add, far_sums)
        sums = jnp.where(
            near == 0, jnp.stack([near_sum, far_sum]), jnp.stack([far_sum, near_sum])
        )
    else:
        acts_all = lax.all_gather(hidden, "narrow", axis=0, tiled=True)
        all_grads = lax.all_gather(out_grad.T, "wide", axis=0, tiled=True)
        tokens = out_grad.shape[0]
        sums = jnp.stack(
            [
                piece(
                    middle,
                    groups,
                    scalars(1, 0, middle),
                    [(acts_all, SEQ, example, middle, 0)],
                    [
                        [
                            (all_grads, tokens, example * (SEQ // tokens) + part)
                            for part in range(SEQ // tokens)
                        ]
                    ],
                    [(sign_bits, middle, 0)],
                    samples,
                )
                for example in range(EXAMPLES)
            ]
        )
    parity = bit_parity(
        jnp.bitwise_and(pick_rows // rows_local, wide_index), wide_count.bit_length() - 1
    ) + bit_parity(
        jnp.bitwise_and(pick_cols // cols_local, narrow_index), narrow_count.bit_length() - 1
    )
    scale = 1.0 / math.sqrt(GROUPS * BAND * cols_local * narrow_count * SEQ)
    weights = (1 - 2 * (parity % 2)).astype(jnp.float32) * scale
    terms = sums.reshape(EXAMPLES, picks) * weights[None]
    return sum_over(sum_over(terms, "wide"), "narrow")


def solution(mesh):
    placed = (P("narrow", "wide"), P("wide", "narrow"), P("wide", "narrow"), P(), P())
    return jax.shard_map(shards, mesh=mesh, in_specs=placed, out_specs=P(), check_vma=False)
```
